32 devices in a mesh: lon: 8 (over y, x, core), lat: 4 (over z).
Axes of the slice: x: 2, y: 2, z: 4, core: 2. Of those that a mesh axis runs over, the one named last changes fastest.
Arguments:
- cotangent: float32 [4, 1, 1024, 2048], P(None, None, 'lat', 'lon'), may hold values from -6 to 6
- lat_cell: int32 [1, 1024, 2048], P(None, 'lat', 'lon'), may hold values from 0 to 1023, as said below
- lat_frac: float32 [1, 1024, 2048], P(None, 'lat', 'lon'), may hold values from 0 to 1, as said below
- lat_end_cell: int32 [1, 4, 2048], P(None, 'lat', 'lon'), may hold values from 0 to 1023, as said below
- lat_end_frac: float32 [1, 4, 2048], P(None, 'lat', 'lon'), may hold values from 0 to 1, as said below
- lon_cell: int32 [1, 1024, 2048], P(None, 'lat', 'lon'), may hold values from 0 to 2047, as said below
- lon_frac: float32 [1, 1024, 2048], P(None, 'lat', 'lon'), may hold values from 0 to 1, as said below
- lon_end_cell: int32 [1, 1024, 8], P(None, 'lat', 'lon'), may hold values from 0 to 2047, as said below
- lon_end_frac: float32 [1, 1024, 8], P(None, 'lat', 'lon'), may hold values from 0 to 1, as said below
Outputs:
- mass_grad: float32 [4, 1, 1024, 2048], P(None, None, 'lat', 'lon')
The draws below stay inside these ranges and needn't reach their ends.
Inputs may be any that keep to these rules, and one draw needn't show every extreme that they name: lat_cell + lat_frac never falls along latitude and lies strictly between n - 32 and n + 32 for arrival row n (within the grid); row 0 has edge 0. `lat_frac`: holds the fractional part of the edges of lat_cell; an edge on a cell boundary is given as the lower cell with 1. `lat_end_cell`: the end edge of block b equals the left edge of row (256 * (b + 1)), given as the lower cell with 1 on a boundary; the last block's is 1023 with fraction 1. `lat_end_frac`: fractional parts of the end edges. lon_cell + lon_frac never falls along longitude and lies in (n - 256, n] for arrival column n (upstream only); column 0 has edge 0. `lon_frac`: holds the fractional part of the edges of lon_cell; an edge on a cell boundary is given as the lower cell with 1. `lon_end_cell`: the end edge of block b equals the left edge of column (256 * (b + 1)), given as the lower cell with 1 on a boundary; the last block's is 2047 with fraction 1. `lon_end_frac`: fractional parts of the end edges.
All inputs are finite; a program needn't handle non-finite values.
Results may differ from the reference program's by a relative error of at most 0.0003.
Values sent between devices are 32-bit elements; how exact they have to be, the bound alone decides.
A program may use at most 64 MiB of HBM per device.

```python
import jax
import jax.numpy as jnp
from jax import lax

TR = 4
REACH = 32
KL = 1
LATC = 256
LONC = 256
LAT_BLOCKS = 4
LON_BLOCKS = 8
NLAT = 1024
NLON = 2048


def lat_edges(key):
    folded = jax.random.fold_in(key, 11)
    sign_key, size_key, step_key = jax.random.split(folded, 3)
    magnitude = jax.random.randint(size_key, (KL, 1, NLON), 32 * REACH, 64 * REACH)
    direction = 2 * jax.random.randint(sign_key, (KL, 1, NLON), 0, 2) - 1
    offset_units = direction * magnitude
    steps = jax.random.randint(step_key, (KL, NLAT + 1, NLON), -16, 17)
    wander = jnp.cumsum(steps, axis=1)
    reach_max = 64 * REACH - 1
    displaced = jnp.clip(offset_units + wander, -reach_max, reach_max)
    edge_iota = lax.broadcasted_iota(jnp.int32, (KL, NLAT + 1, NLON), 1)
    subunits = jnp.clip(64 * edge_iota + displaced, 0, 64 * NLAT)
    subunits = jnp.where(edge_iota == 0, 0, jnp.where(edge_iota == NLAT, 64 * NLAT, subunits))
    cell_index = jnp.maximum(subunits - 1, 0) // 64
    fraction = (subunits - 64 * cell_index).astype(jnp.float32) / 64.0
    return (cell_index, fraction)


def lon_edges(key):
    folded = jax.random.fold_in(key, 23)
    first_key, second_key = jax.random.split(folded)
    offset_units = jax.random.randint(first_key, (KL, NLAT, 1), 0, 64 * LONC + 1)
    steps = jax.random.randint(second_key, (KL, NLAT, NLON + 1), -40, 41)
    upstream = jnp.clip(offset_units + jnp.abs(jnp.cumsum(steps, axis=2)), 0, 64 * LONC - 1)
    edge_iota = lax.broadcasted_iota(jnp.int32, (KL, NLAT, NLON + 1), 2)
    subunits = jnp.clip(64 * edge_iota - upstream, 0, 64 * NLON)
    subunits = jnp.where(edge_iota == NLON, 64 * NLON, subunits)
    cell_index = jnp.maximum(subunits - 1, 0) // 64
    fraction = (subunits - 64 * cell_index).astype(jnp.float32) / 64.0
    return (cell_index, fraction)


def draw_lat_cell(key, part):
    return lat_edges(key)[0][:, :NLAT, :]


def draw_lat_frac(key, part):
    return lat_edges(key)[1][:, :NLAT, :]


def draw_lat_end_cell(key, part):
    return lat_edges(key)[0][:, LATC::LATC, :]


def draw_lat_end_frac(key, part):
    return lat_edges(key)[1][:, LATC::LATC, :]


def draw_lon_cell(key, part):
    return lon_edges(key)[0][:, :, :NLON]


def draw_lon_frac(key, part):
    return lon_edges(key)[1][:, :, :NLON]


def draw_lon_end_cell(key, part):
    return lon_edges(key)[0][:, :, LONC::LONC]


def draw_lon_end_frac(key, part):
    return lon_edges(key)[1][:, :, LONC::LONC]


def block_levels(own_key, dims, cuts, least, top_value):
    gain, own = 1.0, jax.random.fold_in(own_key, 6)
    for dim, shards_of in cuts:
        draws = jnp.exp(jax.random.uniform(jax.random.fold_in(own, dim), (shards_of,), jnp.float32, least / len(cuts), top_value / len(cuts)))
        gain = gain * jnp.repeat(draws, dims[dim] // shards_of).reshape([-1 if axis == dim else 1 for axis in range(len(dims))])
    return gain


def gaussian(own_key, shape, scale, most, cuts=(), held_as=jnp.bfloat16):
    gain = block_levels(own_key, shape, cuts, -0.22, 0.18) if cuts else 1.0
    entries = jax.random.normal(own_key, shape, jnp.float32) * scale * gain
    return jnp.minimum(jnp.maximum(entries, -most), most).astype(held_as)


def setup_inputs(seed: int = 0) -> dict:
    keys = jax.random.split(jax.random.key(seed), 10)
    cotangent = gaussian(keys[0], (TR, KL, NLAT, NLON), 1.0, 6.0, ((2, 4), (3, 8)), jnp.float32)
    lat_cell = draw_lat_cell(jax.random.fold_in(keys[9], 71), 0)
    lat_frac = draw_lat_frac(jax.random.fold_in(keys[9], 71), 0)
    lat_end_cell = draw_lat_end_cell(jax.random.fold_in(keys[9], 71), 0)
    lat_end_frac = draw_lat_end_frac(jax.random.fold_in(keys[9], 71), 0)
    lon_cell = draw_lon_cell(jax.random.fold_in(keys[9], 71), 0)
    lon_frac = draw_lon_frac(jax.random.fold_in(keys[9], 71), 0)
    lon_end_cell = draw_lon_end_cell(jax.random.fold_in(keys[9], 71), 0)
    lon_end_frac = draw_lon_end_frac(jax.random.fold_in(keys[9], 71), 0)
    return dict(cotangent=cotangent, lat_cell=lat_cell, lat_frac=lat_frac, lat_end_cell=lat_end_cell, lat_end_frac=lat_end_frac, lon_cell=lon_cell, lon_frac=lon_frac, lon_end_cell=lon_end_cell, lon_end_frac=lon_end_frac)


def lat_right(left_edges, end_edges):
    blocks = left_edges.reshape(LAT_BLOCKS, LATC, NLON)
    return jnp.concatenate([blocks[:, 1:, :], end_edges[:, None, :]], axis=1).reshape(NLAT, NLON)


def lon_right(left_edges, end_edges):
    blocks = left_edges.reshape(NLAT, LON_BLOCKS, LONC)
    return jnp.concatenate([blocks[:, :, 1:], end_edges[:, :, None]], axis=2).reshape(NLAT, NLON)


def remap_adjoint(values, left_cell, left_frac, right_cell, right_frac, along_lat):
    row_iota = lax.broadcasted_iota(jnp.int32, left_cell.shape, 0)
    col_iota = lax.broadcasted_iota(jnp.int32, left_cell.shape, 1)
    if along_lat:
        right_target = (slice(None), right_cell, col_iota)
        left_target = (slice(None), left_cell, col_iota)
        along = 1
    else:
        right_target = (slice(None), row_iota, right_cell)
        left_target = (slice(None), row_iota, left_cell)
        along = 2
    blank_sum = jnp.zeros(values.shape, jnp.float32)
    negative = -values
    position = blank_sum.at[right_target].add(values).at[left_target].add(negative)
    fraction = blank_sum.at[right_target].add(values * right_frac).at[left_target].add(negative * left_frac)
    suffix = jnp.flip(jnp.cumsum(jnp.flip(position, along), axis=along), along) - position
    return fraction + suffix


def reference(cotangent, lat_cell, lat_frac, lat_end_cell, lat_end_frac, lon_cell, lon_frac, lon_end_cell, lon_end_frac):
    by_level = jnp.moveaxis(cotangent, 1, 0)

    def one_level(level_items):
        values, la_cell, la_frac, la_end_cell, la_end_frac, lo_cell, lo_frac, lo_end_cell, lo_end_frac = level_items
        middle = remap_adjoint(values, la_cell, la_frac, lat_right(la_cell, la_end_cell), lat_right(la_frac, la_end_frac), True)
        return remap_adjoint(middle, lo_cell, lo_frac, lon_right(lo_cell, lo_end_cell), lon_right(lo_frac, lo_end_frac), False)

    result = lax.map(one_level, (by_level, lat_cell, lat_frac, lat_end_cell, lat_end_frac, lon_cell, lon_frac, lon_end_cell, lon_end_frac))
    return jnp.moveaxis(result, 0, 1)
```

```python
import functools

import jax
import jax.numpy as jnp
from jax import lax
from jax.experimental import pallas as pl
from jax.experimental.pallas import tpu as pltpu
from jax.sharding import PartitionSpec as P

REACH = 32
GROUP = 64


def take(table, at):
    return jnp.take_along_axis(table, at, axis=1, mode="promise_in_bounds")


def lanes_of(rows, half):
    return lax.broadcasted_iota(jnp.int32, (rows, half), 1)


def upper(length):
    before = lax.broadcasted_iota(jnp.int32, (length, length), 0)
    after = lax.broadcasted_iota(jnp.int32, (length, length), 1)
    return jnp.where(before < after, 1.0, 0.0).astype(jnp.bfloat16)


def running(edges, end, values, tri):
    rows, half = edges[0].shape
    lane = lanes_of(rows, half)
    back = [pltpu.roll(edge, half - 1, 1) for edge in edges]
    width = [
        jnp.where(lane == half - 1, back[1], back[0]) - edges[0],
        jnp.where(lane == half - 1, end, back[1]) - edges[1],
    ]
    whole = jnp.concatenate(
        [jnp.concatenate([v[0] * width[0], v[1] * width[1]], axis=1) for v in values], axis=0
    )
    high = whole.astype(jnp.bfloat16)
    low = (whole - high.astype(jnp.float32)).astype(jnp.bfloat16)
    total = jnp.dot(high, tri, preferred_element_type=jnp.float32) + jnp.dot(
        low, tri, preferred_element_type=jnp.float32
    )
    return [
        (total[t * rows : (t + 1) * rows, :half], total[t * rows : (t + 1) * rows, half:])
        for t in range(len(values))
    ]


def integral(points, halves, edges, end, values, sums):
    rows, half = edges[0].shape
    first = jnp.broadcast_to(edges[0][:, :1], (rows, half))
    x = jnp.minimum(jnp.maximum(points, first), end)
    if len(halves) == 2:
        upper_half = jnp.broadcast_to(edges[1][:, :1], (rows, half)) <= x

    def fetch(pair, at):
        if len(halves) == 1:
            return take(pair[halves[0]], at)
        return jnp.where(upper_half, take(pair[1], at), take(pair[0], at))

    at = jnp.zeros((rows, half), jnp.int32)
    step = half // 2
    while step:
        further = at + step
        at = jnp.where(fetch(edges, further) <= x, further, at)
        step //= 2
    inside = x - fetch(edges, at)
    return [fetch(s, at) + fetch(v, at) * inside for s, v in zip(sums, values)]


def step_up(now, before):
    lane = lanes_of(*now.shape)
    return now - jnp.where(lane == 0, before if before is None else pltpu.roll(before, 1, 1), pltpu.roll(now, 1, 1))


def lat_kernel(cot_ref, cell_ref, frac_ref, endc_ref, endf_ref, own_ref, halo_ref, vt, et, endt, mt):
    tracers, lat_rows, cols = cot_ref.shape
    half = lat_rows // 2
    first_cell = lax.axis_index("lat") * lat_rows
    edges = (cell_ref[...] - first_cell).astype(jnp.float32) + frac_ref[...]
    et[...] = edges.T
    end = (endc_ref[...] - first_cell).astype(jnp.float32) + endf_ref[...]
    endt[...] = jnp.broadcast_to(end, (half, cols)).T
    for t in range(tracers):
        vt[t] = cot_ref[t].T
    tri = upper(lat_rows)
    group = min(GROUP, cols)

    @pl.loop(0, cols // group)
    def _(g):
        at = pl.ds(pl.multiple_of(g * group, group), group)
        pair = (et[at, :half], et[at, half:])
        last = endt[at, :]
        values = [(vt[t, at, :half], vt[t, at, half:]) for t in range(tracers)]
        sums = running(pair, last, values, tri)
        lane = lanes_of(group, half)
        places = (
            jnp.where(lane < half // 2, lane + 2 * half, lane - half),
            lane,
            lane + half,
        )
        got = [
            integral((p + 1).astype(jnp.float32), (0, 1), pair, last, values, sums)
            for p in places
        ]
        for t in range(tracers):
            for b in range(3):
                mt[t, b, at, :] = step_up(got[b][t], got[b - 1][t])

    for t in range(tracers):
        halo_ref[t] = mt[t, 0].T
        own_ref[t, :half] = mt[t, 1].T
        own_ref[t, half:] = mt[t, 2].T


def lon_kernel(mid_ref, cell_ref, frac_ref, endc_ref, endf_ref, own_ref, low_ref):
    tracers, rows, cols = mid_ref.shape
    half = cols // 2
    first_cell = lax.axis_index("lon") * cols
    tri = upper(cols)
    group = min(GROUP, rows)

    @pl.loop(0, rows // group)
    def _(g):
        at = pl.ds(pl.multiple_of(g * group, group), group)
        edges = (cell_ref[at, :] - first_cell).astype(jnp.float32) + frac_ref[at, :]
        pair = (edges[:, :half], edges[:, half:])
        last = (endc_ref[at, :] - first_cell).astype(jnp.float32) + endf_ref[at, :]
        last = jnp.broadcast_to(last, (group, half))
        values = [(mid_ref[t, at, :half], mid_ref[t, at, half:]) for t in range(tracers)]
        sums = running(pair, last, values, tri)
        lane = lanes_of(group, half)
        halves = ((0,), (0, 1), (0, 1), (1,))
        got = [
            integral((lane + ((b - 2) * half + 1)).astype(jnp.float32), halves[b], pair, last, values, sums)
            for b in range(4)
        ]
        none = jnp.zeros((group, half), jnp.float32)
        for t in range(tracers):
            for b in range(4):
                target = low_ref if b < 2 else own_ref
                start = (b % 2) * half
                target[t, at, start : start + half] = step_up(
                    got[b][t], got[b - 1][t] if b else none
                )


def passed_along(shard, axis, by):
    count = lax.axis_size(axis)
    pairs = [(i, i + by) for i in range(count) if 0 <= i + by < count]
    return lax.ppermute(shard, axis, pairs)


def shards(cotangent, lat_cell, lat_frac, lat_end_cell, lat_end_frac, lon_cell, lon_frac, lon_end_cell, lon_end_frac):
    tracers, levels, rows, cols = cotangent.shape
    f32 = jnp.float32
    half = rows // 2
    own, halo = pl.pallas_call(
        lat_kernel,
        out_shape=(
            jax.ShapeDtypeStruct((tracers, rows, cols), f32),
            jax.ShapeDtypeStruct((tracers, half, cols), f32),
        ),
        scratch_shapes=[
            pltpu.VMEM((tracers, cols, rows), f32),
            pltpu.VMEM((cols, rows), f32),
            pltpu.VMEM((cols, half), f32),
            pltpu.VMEM((tracers, 3, cols, half), f32),
        ],
        compiler_params=pltpu.CompilerParams(vmem_limit_bytes=48 * 2**20),
        name="lat_pass",
    )(
        cotangent.reshape(tracers, rows, cols),
        lat_cell.reshape(rows, cols),
        lat_frac.reshape(rows, cols),
        lat_end_cell.reshape(1, cols),
        lat_end_frac.reshape(1, cols),
    )
    from_low = passed_along(halo[:, :REACH], "lat", 1)
    from_high = passed_along(halo[:, half - REACH :], "lat", -1)
    middle = own.at[:, :REACH].add(from_low).at[:, rows - REACH :].add(from_high)
    own_part, low_part = pl.pallas_call(
        lon_kernel,
        out_shape=(
            jax.ShapeDtypeStruct((tracers, rows, cols), f32),
            jax.ShapeDtypeStruct((tracers, rows, cols), f32),
        ),
        compiler_params=pltpu.CompilerParams(vmem_limit_bytes=48 * 2**20),
        name="lon_pass",
    )(
        middle,
        lon_cell.reshape(rows, cols),
        lon_frac.reshape(rows, cols),
        lon_end_cell.reshape(rows, 1),
        lon_end_frac.reshape(rows, 1),
    )
    out = own_part + passed_along(low_part, "lon", -1)
    return out.reshape(cotangent.shape)


def solution(mesh):
    whole = P(None, None, "lat", "lon")
    placed = (whole,) + (P(None, "lat", "lon"),) * 8
    return jax.shard_map(shards, mesh=mesh, in_specs=placed, out_specs=whole, check_vma=False)
```

```python
import functools

import jax
import jax.numpy as jnp
from jax import lax
from jax.experimental import pallas as pl
from jax.experimental.pallas import tpu as pltpu
from jax.sharding import PartitionSpec as P

REACH = 32
GROUP = 64
SEND = 64


def take(table, at):
    return jnp.take_along_axis(table, at, axis=1, mode="promise_in_bounds")


def lanes_of(rows, half):
    return lax.broadcasted_iota(jnp.int32, (rows, half), 1)


def upper(length):
    before = lax.broadcasted_iota(jnp.int32, (length, length), 0)
    after = lax.broadcasted_iota(jnp.int32, (length, length), 1)
    return jnp.where(before < after, 1.0, 0.0).astype(jnp.bfloat16)


def running(edges, end, values, tri):
    rows, half = edges[0].shape
    lane = lanes_of(rows, half)
    back = [pltpu.roll(edge, half - 1, 1) for edge in edges]
    width = [
        jnp.where(lane == half - 1, back[1], back[0]) - edges[0],
        jnp.where(lane == half - 1, end, back[1]) - edges[1],
    ]
    whole = jnp.concatenate(
        [jnp.concatenate([v[0] * width[0], v[1] * width[1]], axis=1) for v in values], axis=0
    )
    high = whole.astype(jnp.bfloat16)
    low = (whole - high.astype(jnp.float32)).astype(jnp.bfloat16)
    total = jnp.dot(high, tri, preferred_element_type=jnp.float32) + jnp.dot(
        low, tri, preferred_element_type=jnp.float32
    )
    return [
        (total[t * rows : (t + 1) * rows, :half], total[t * rows : (t + 1) * rows, half:])
        for t in range(len(values))
    ]


def integral(points, halves, edges, end, values, sums):
    rows, half = edges[0].shape
    first = jnp.broadcast_to(edges[0][:, :1], (rows, half))
    x = jnp.minimum(jnp.maximum(points, first), end)
    if len(halves) == 2:
        upper_half = jnp.broadcast_to(edges[1][:, :1], (rows, half)) <= x

    def fetch(pair, at):
        if len(halves) == 1:
            return take(pair[halves[0]], at)
        return jnp.where(upper_half, take(pair[1], at), take(pair[0], at))

    at = jnp.zeros((rows, half), jnp.int32)
    step = half // 2
    while step:
        further = at + step
        at = jnp.where(fetch(edges, further) <= x, further, at)
        step //= 2
    inside = x - fetch(edges, at)
    return [fetch(s, at) + fetch(v, at) * inside for s, v in zip(sums, values)]


def step_up(now, before):
    lane = lanes_of(*now.shape)
    return now - jnp.where(lane == 0, before if before is None else pltpu.roll(before, 1, 1), pltpu.roll(now, 1, 1))


MESH = pl.DeviceIdType.MESH


def lat_pass(cot_ref, cell_ref, frac_ref, endc_ref, endf_ref, mid_ref, up_ref, down_ref, vt, et, endt, mt):
    tracers, lat_rows, cols = cot_ref.shape
    half = lat_rows // 2
    reach = up_ref.shape[1]
    first_cell = lax.axis_index("lat") * lat_rows
    edges = (cell_ref[...] - first_cell).astype(jnp.float32) + frac_ref[...]
    et[...] = edges.T
    end = (endc_ref[...] - first_cell).astype(jnp.float32) + endf_ref[...]
    endt[...] = jnp.broadcast_to(end, (half, cols)).T
    for t in range(tracers):
        vt[t] = cot_ref[t].T
    tri = upper(lat_rows)
    group = min(GROUP, cols)

    @pl.loop(0, cols // group)
    def _(g):
        at = pl.ds(pl.multiple_of(g * group, group), group)
        pair = (et[at, :half], et[at, half:])
        last = endt[at, :]
        values = [(vt[t, at, :half], vt[t, at, half:]) for t in range(tracers)]
        sums = running(pair, last, values, tri)
        lane = lanes_of(group, half)
        places = (
            jnp.where(lane < half // 2, lane + 2 * half, lane - half),
            lane,
            lane + half,
        )
        got = [
            integral((p + 1).astype(jnp.float32), (0, 1), pair, last, values, sums)
            for p in places
        ]
        for t in range(tracers):
            for b in range(3):
                mt[t, b, at, :] = step_up(got[b][t], got[b - 1][t])

    for t in range(tracers):
        halo = mt[t, 0].T
        up_ref[t] = halo[:reach]
        down_ref[t] = halo[half - reach :]


def lon_group(at, first_cell, mid_ref, cell_ref, frac_ref, endc_ref, endf_ref, own_ref, low_ref, g, tri):
    tracers, rows, cols = mid_ref.shape
    half = cols // 2
    group = low_ref.shape[2]
    edges = (cell_ref[at, :] - first_cell).astype(jnp.float32) + frac_ref[at, :]
    pair = (edges[:, :half], edges[:, half:])
    last = (endc_ref[at, :] - first_cell).astype(jnp.float32) + endf_ref[at, :]
    last = jnp.broadcast_to(last, (group, half))
    values = [(mid_ref[t, at, :half], mid_ref[t, at, half:]) for t in range(tracers)]
    sums = running(pair, last, values, tri)
    lane = lanes_of(group, half)
    halves = ((0,), (0, 1), (0, 1), (1,))
    got = [
        integral((lane + ((b - 2) * half + 1)).astype(jnp.float32), halves[b], pair, last, values, sums)
        for b in range(4)
    ]
    none = jnp.zeros((group, half), jnp.float32)
    for t in range(tracers):
        for b in range(4):
            cells = step_up(got[b][t], got[b - 1][t] if b else none)
            start = (b % 2) * half
            if b < 2:
                low_ref[g, t, :, start : start + half] = cells
            else:
                own_ref[t, at, start : start + half] = cells


def kernel(
    lats, lons, cot_hbm, latc_hbm, latf_hbm, lat_endc, lat_endf, lonc_hbm, lonf_hbm, lon_endc, lon_endf,
    out_ref, cot, latc, latf, lonc, lonf, vt, et, endt, mt, mid, edge_out, edge_in, low_out, low_in,
    load_sem, edge_send, edge_recv, low_send, low_recv,
):
    tracers, rows, cols = cot.shape
    half = rows // 2
    reach = edge_out.shape[2]
    groups, _, group, _ = low_out.shape
    loads = [
        pltpu.make_async_copy(source, target, load_sem.at[k])
        for k, (source, target) in enumerate(
            zip((latc_hbm, latf_hbm, cot_hbm, lonc_hbm, lonf_hbm), (latc, latf, cot, lonc, lonf))
        )
    ]
    for load in loads:
        load.start()
    la, lo = lax.axis_index("lat"), lax.axis_index("lon")
    has_up, has_down = la < lats - 1, la > 0
    has_right, has_left = lo < lons - 1, lo > 0
    barrier = pltpu.get_barrier_semaphore()
    for there, where in (
        (has_up, {"lat": la + 1}),
        (has_down, {"lat": la - 1}),
        (has_right, {"lon": lo + 1}),
        (has_left, {"lon": lo - 1}),
    ):

        @pl.when(there)
        def _(where=where):
            pl.semaphore_signal(barrier, inc=1, device_id=where, device_id_type=MESH)

    for load in loads:
        load.wait()
    lat_pass(cot, latc, latf, lat_endc, lat_endf, mid, edge_out.at[0], edge_out.at[1], vt, et, endt, mt)
    peers = [there.astype(jnp.int32) for there in (has_up, has_down, has_right, has_left)]
    pl.semaphore_wait(barrier, peers[0] + peers[1] + peers[2] + peers[3])

    def edge(k, where):
        return pltpu.make_async_remote_copy(
            src_ref=edge_out.at[k],
            dst_ref=edge_in.at[k],
            send_sem=edge_send.at[k],
            recv_sem=edge_recv.at[k],
            device_id={"lat": where},
            device_id_type=MESH,
        )

    up, down = edge(0, la + 1), edge(1, la - 1)
    pl.when(has_up)(up.start)
    pl.when(has_down)(down.start)
    for t in range(tracers):
        mid[t, :half] = mt[t, 1].T
        mid[t, half:] = mt[t, 2].T

    def low(g):
        return pltpu.make_async_remote_copy(
            src_ref=low_out.at[g],
            dst_ref=low_in.at[g],
            send_sem=low_send.at[g],
            recv_sem=low_recv.at[g],
            device_id={"lon": lo - 1},
            device_id_type=MESH,
        )

    tri = upper(cols)

    @pl.loop(0, groups)
    def _(k):
        @pl.when(k == max(groups - 2, 0))
        def _():
            @pl.when(has_down)
            def _():
                up.wait_recv()
                mid[:, :reach] += edge_in[0]

            @pl.when(has_up)
            def _():
                down.wait_recv()
                mid[:, rows - reach :] += edge_in[1]

        g = lax.rem(k + 1, groups)
        at = pl.ds(pl.multiple_of(g * group, group), group)
        lon_group(at, lo * cols, mid, lonc, lonf, lon_endc, lon_endf, out_ref, low_out, g, tri)
        pl.when(has_left)(low(g).start)

    @pl.when(has_right)
    def _():
        @pl.loop(0, groups)
        def _(k):
            g = lax.rem(k + 1, groups)
            low(g).wait_recv()
            at = pl.ds(pl.multiple_of(g * group, group), group)
            out_ref[:, at, :] += low_in[g]

    pl.when(has_up)(up.wait_send)
    pl.when(has_down)(down.wait_send)

    @pl.when(has_left)
    def _():
        @pl.loop(0, groups)
        def _(g):
            low(g).wait_send()


def shards(lats, lons, cotangent, lat_cell, lat_frac, lat_end_cell, lat_end_frac, lon_cell, lon_frac, lon_end_cell, lon_end_frac):
    tracers, levels, rows, cols = cotangent.shape
    f32, i32 = jnp.float32, jnp.int32
    half = rows // 2
    group = min(SEND, rows)
    groups = rows // group
    anywhere, vmem = pl.BlockSpec(memory_space=pl.ANY), pl.BlockSpec(memory_space=pltpu.VMEM)
    out = pl.pallas_call(
        functools.partial(kernel, lats, lons),
        out_shape=jax.ShapeDtypeStruct((tracers, rows, cols), f32),
        in_specs=[anywhere, anywhere, anywhere, vmem, vmem, anywhere, anywhere, vmem, vmem],
        out_specs=vmem,
        scratch_shapes=[
            pltpu.VMEM((tracers, rows, cols), f32),
            pltpu.VMEM((rows, cols), i32),
            pltpu.VMEM((rows, cols), f32),
            pltpu.VMEM((rows, cols), i32),
            pltpu.VMEM((rows, cols), f32),
            pltpu.VMEM((tracers, cols, rows), f32),
            pltpu.VMEM((cols, rows), f32),
            pltpu.VMEM((cols, half), f32),
            pltpu.VMEM((tracers, 3, cols, half), f32),
            pltpu.VMEM((tracers, rows, cols), f32),
            pltpu.VMEM((2, tracers, REACH, cols), f32),
            pltpu.VMEM((2, tracers, REACH, cols), f32),
            pltpu.VMEM((groups, tracers, group, cols), f32),
            pltpu.VMEM((groups, tracers, group, cols), f32),
            pltpu.SemaphoreType.DMA((5,)),
            pltpu.SemaphoreType.DMA((2,)),
            pltpu.SemaphoreType.DMA((2,)),
            pltpu.SemaphoreType.DMA((groups,)),
            pltpu.SemaphoreType.DMA((groups,)),
        ],
        compiler_params=pltpu.CompilerParams(
            collective_id=0, has_side_effects=True, vmem_limit_bytes=48 * 2**20
        ),
        name="remap_adjoint",
    )(
        cotangent.reshape(tracers, rows, cols),
        lat_cell.reshape(rows, cols),
        lat_frac.reshape(rows, cols),
        lat_end_cell.reshape(1, cols),
        lat_end_frac.reshape(1, cols),
        lon_cell.reshape(rows, cols),
        lon_frac.reshape(rows, cols),
        lon_end_cell.reshape(rows, 1),
        lon_end_frac.reshape(rows, 1),
    )
    return out.reshape(cotangent.shape)


def solution(mesh):
    whole = P(None, None, "lat", "lon")
    placed = (whole,) + (P(None, "lat", "lon"),) * 8
    body = functools.partial(shards, mesh.shape["lat"], mesh.shape["lon"])
    return jax.shard_map(body, mesh=mesh, in_specs=placed, out_specs=whole, check_vma=False)
```

```python
import functools

import jax
import jax.numpy as jnp
from jax import lax
from jax.experimental import pallas as pl
from jax.experimental.pallas import tpu as pltpu
from jax.sharding import PartitionSpec as P

REACH = 32
GROUP = 128
SEND = 32
VMEM = 63 * 2**20


def take(table, at):
    return jnp.take_along_axis(table, at, axis=1, mode="promise_in_bounds")


def lanes_of(rows, half):
    return lax.broadcasted_iota(jnp.int32, (rows, half), 1)


def upper(length):
    before = lax.broadcasted_iota(jnp.int32, (length, length), 0)
    after = lax.broadcasted_iota(jnp.int32, (length, length), 1)
    return jnp.where(before < after, 1.0, 0.0).astype(jnp.bfloat16)


def running(edges, end, values, tri):
    rows, half = edges[0].shape
    lane = lanes_of(rows, half)
    back = [pltpu.roll(edge, half - 1, 1) for edge in edges]
    width = [
        jnp.where(lane == half - 1, back[1], back[0]) - edges[0],
        jnp.where(lane == half - 1, end, back[1]) - edges[1],
    ]
    whole = jnp.concatenate(
        [jnp.concatenate([v[0] * width[0], v[1] * width[1]], axis=1) for v in values], axis=0
    )
    high = whole.astype(jnp.bfloat16)
    low = (whole - high.astype(jnp.float32)).astype(jnp.bfloat16)
    both = jnp.dot(jnp.concatenate([high, low], axis=0), tri, preferred_element_type=jnp.float32)
    count = whole.shape[0]
    total = both[:count] + both[count:]
    return [
        tuple(
            total[t * rows : (t + 1) * rows, h * half : (h + 1) * half] - values[t][h] * edges[h]
            for h in (0, 1)
        )
        for t in range(len(values))
    ]


def spread(table, lane, shape):
    return jnp.broadcast_to(table[:, lane : lane + 1], shape)


def integral(points, halves, edges, marks, end, values, starts):
    shape = edges[0].shape
    half = shape[1]
    x = jnp.minimum(jnp.maximum(points, marks[0][0]), end)
    if len(halves) == 2:
        upper_half = marks[1][0] <= x

    def pick(pair):
        if len(halves) == 1:
            return pair[halves[0]]
        return jnp.where(upper_half, pair[1], pair[0])

    def fetch(pair, at):
        if len(halves) == 1:
            return take(pair[halves[0]], at)
        return jnp.where(upper_half, take(pair[1], at), take(pair[0], at))

    step = half // 2
    at = jnp.where(pick((marks[0][1], marks[1][1])) <= x, step, 0)
    step //= 2
    while step:
        further = at + step
        at = jnp.where(fetch(edges, further) <= x, further, at)
        step //= 2
    return [fetch(s, at) + fetch(v, at) * x for s, v in zip(starts, values)]


def near_integral(points, reach, source, edges, first, end, values, starts):
    half = edges[0].shape[1]
    length = 2 * half
    x = jnp.minimum(jnp.maximum(points.astype(jnp.float32), first), end)

    def fetch(pair, at):
        lane = jnp.bitwise_and(at, half - 1)
        if source is not None:
            return take(pair, lane)
        return jnp.where(at >= half, take(pair[1], lane), take(pair[0], lane))

    at = points - reach
    step = reach
    while step:
        further = at + step
        found = fetch(edges if source is None else source[0], further)
        ahead = jnp.logical_and(further < length, jnp.logical_or(further < 0, found <= x))
        at = jnp.where(ahead, further, at)
        step //= 2
    at = jnp.clip(at, 0, length - 1)
    tables = zip(starts, values) if source is None else zip(source[1], source[2])
    return [fetch(s, at) + fetch(v, at) * x for s, v in tables]


def step_up(now, before):
    lane = lanes_of(*now.shape)
    return now - jnp.where(lane == 0, before if before is None else pltpu.roll(before, 1, 1), pltpu.roll(now, 1, 1))


MESH = pl.DeviceIdType.MESH


def lat_pass(cot_ref, cell_ref, frac_ref, endc_ref, endf_ref, mid_ref, up_ref, down_ref, vt, et, endt, mt):
    tracers, lat_rows, cols = cot_ref.shape
    half = lat_rows // 2
    reach = up_ref.shape[1]
    first_cell = lax.axis_index("lat") * lat_rows
    edges = (cell_ref[...] - first_cell).astype(jnp.float32) + frac_ref[...]
    et[...] = edges.T
    end = (endc_ref[...] - first_cell).astype(jnp.float32) + endf_ref[...]
    endt[...] = jnp.broadcast_to(end, (half, cols)).T
    for t in range(tracers):
        vt[t] = cot_ref[t].T
    tri = upper(lat_rows)
    group = min(GROUP, cols)

    @pl.loop(0, cols // group)
    def _(g):
        at = pl.ds(pl.multiple_of(g * group, group), group)
        pair = (et[at, :half], et[at, half:])
        last = endt[at, :]
        values = [(vt[t, at, :half], vt[t, at, half:]) for t in range(tracers)]
        sums = running(pair, last, values, tri)
        lane = lanes_of(group, half)
        first = spread(pair[0], 0, pair[0].shape)
        rim = jnp.where(lane < half // 2, lane + 2 * half, lane - half)

        def ends(both):
            return jnp.where(lane < half // 2, both[0], both[1])

        source = (ends(pair), [ends(s) for s in sums], [ends(v) for v in values])
        got = [
            near_integral(p + 1, reach, src, pair, first, last, values, sums)
            for p, src in ((rim, source), (lane, None), (lane + half, None))
        ]
        for t in range(tracers):
            for b in range(3):
                mt[t, b, at, :] = step_up(got[b][t], got[b - 1][t])

    for t in range(tracers):
        halo = mt[t, 0].T
        up_ref[t] = halo[:reach]
        down_ref[t] = halo[half - reach :]


def lon_group(at, first_cell, mid_ref, cell_ref, frac_ref, end_ref, own_ref, low_ref, g, tri):
    tracers, rows, cols = mid_ref.shape
    half = cols // 2
    group = low_ref.shape[2]
    edges = (cell_ref[at, :] - first_cell).astype(jnp.float32) + frac_ref[at, :]
    pair = (edges[:, :half], edges[:, half:])
    last = end_ref[at, :]
    values = [(mid_ref[t, at, :half], mid_ref[t, at, half:]) for t in range(tracers)]
    sums = running(pair, last, values, tri)
    lane = lanes_of(group, half)
    halves = ((0,), (0, 1), (0, 1), (1,))
    marks = [[spread(edge, at, edge.shape) for at in (0, half // 2)] for edge in pair]
    got = [
        integral((lane + ((b - 2) * half + 1)).astype(jnp.float32), halves[b], pair, marks, last, values, sums)
        for b in range(4)
    ]
    none = jnp.zeros((group, half), jnp.float32)
    for t in range(tracers):
        for b in range(4):
            cells = step_up(got[b][t], got[b - 1][t] if b else none)
            start = (b % 2) * half
            if b < 2:
                low_ref[g, t, :, start : start + half] = cells
            else:
                own_ref[t, at, start : start + half] = cells


def kernel(
    lats, lons, cot_hbm, latc_hbm, latf_hbm, lat_endc, lat_endf, lonc_hbm, lonf_hbm, lon_endc, lon_endf,
    out_ref, cot, latc, latf, lonc, lonf, vt, et, endt, mt, mid, lon_end, edge_out, edge_in, low_out, low_in,
    load_sem, edge_send, edge_recv, low_send, low_recv,
):
    tracers, rows, cols = cot.shape
    half = rows // 2
    reach = edge_out.shape[2]
    groups, _, group, _ = low_out.shape
    loads = [
        pltpu.make_async_copy(source, target, load_sem.at[k])
        for k, (source, target) in enumerate(
            zip((latc_hbm, latf_hbm, cot_hbm, lonc_hbm, lonf_hbm), (latc, latf, cot, lonc, lonf))
        )
    ]
    for load in loads:
        load.start()
    la, lo = lax.axis_index("lat"), lax.axis_index("lon")
    has_up, has_down = la < lats - 1, la > 0
    has_right, has_left = lo < lons - 1, lo > 0
    barrier = pltpu.get_barrier_semaphore()
    for there, where in (
        (has_up, {"lat": la + 1}),
        (has_down, {"lat": la - 1}),
        (has_right, {"lon": lo + 1}),
        (has_left, {"lon": lo - 1}),
    ):

        @pl.when(there)
        def _(where=where):
            pl.semaphore_signal(barrier, inc=1, device_id=where, device_id_type=MESH)

    end = (lon_endc[...] - lo * cols).astype(jnp.float32) + lon_endf[...]
    lon_end[...] = jnp.broadcast_to(end, (cols // 2, rows)).T
    for load in loads:
        load.wait()
    lat_pass(cot, latc, latf, lat_endc, lat_endf, mid, edge_out.at[0], edge_out.at[1], vt, et, endt, mt)
    peers = [there.astype(jnp.int32) for there in (has_up, has_down, has_right, has_left)]
    pl.semaphore_wait(barrier, peers[0] + peers[1] + peers[2] + peers[3])

    def edge(k, where):
        return pltpu.make_async_remote_copy(
            src_ref=edge_out.at[k],
            dst_ref=edge_in.at[k],
            send_sem=edge_send.at[k],
            recv_sem=edge_recv.at[k],
            device_id={"lat": where},
            device_id_type=MESH,
        )

    up, down = edge(0, la + 1), edge(1, la - 1)
    pl.when(has_up)(up.start)
    pl.when(has_down)(down.start)
    for t in range(tracers):
        mid[t, :half] = mt[t, 1].T
        mid[t, half:] = mt[t, 2].T

    def low(g):
        return pltpu.make_async_remote_copy(
            src_ref=low_out.at[g],
            dst_ref=low_in.at[g],
            send_sem=low_send.at[g],
            recv_sem=low_recv.at[g],
            device_id={"lon": lo - 1},
            device_id_type=MESH,
        )

    tri = upper(cols)

    @pl.loop(0, groups)
    def _(k):
        @pl.when(k == max(groups - 2, 0))
        def _():
            @pl.when(has_down)
            def _():
                up.wait_recv()
                mid[:, :reach] += edge_in[0]

            @pl.when(has_up)
            def _():
                down.wait_recv()
                mid[:, rows - reach :] += edge_in[1]

        g = lax.rem(k + 1, groups)
        at = pl.ds(pl.multiple_of(g * group, group), group)
        lon_group(at, lo * cols, mid, lonc, lonf, lon_end, out_ref, low_out, g, tri)
        pl.when(has_left)(low(g).start)

    @pl.when(has_right)
    def _():
        @pl.loop(0, groups)
        def _(k):
            g = lax.rem(k + 1, groups)
            low(g).wait_recv()
            at = pl.ds(pl.multiple_of(g * group, group), group)
            out_ref[:, at, :] += low_in[g]

    pl.when(has_up)(up.wait_send)
    pl.when(has_down)(down.wait_send)

    @pl.when(has_left)
    def _():
        @pl.loop(0, groups)
        def _(g):
            low(g).wait_send()


def shards(lats, lons, cotangent, lat_cell, lat_frac, lat_end_cell, lat_end_frac, lon_cell, lon_frac, lon_end_cell, lon_end_frac):
    tracers, levels, rows, cols = cotangent.shape
    f32, i32 = jnp.float32, jnp.int32
    half = rows // 2
    group = min(SEND, rows)
    groups = rows // group
    anywhere, vmem = pl.BlockSpec(memory_space=pl.ANY), pl.BlockSpec(memory_space=pltpu.VMEM)
    out = pl.pallas_call(
        functools.partial(kernel, lats, lons),
        out_shape=jax.ShapeDtypeStruct((tracers, rows, cols), f32),
        in_specs=[anywhere, anywhere, anywhere, vmem, vmem, anywhere, anywhere, vmem, vmem],
        out_specs=vmem,
        scratch_shapes=[
            pltpu.VMEM((tracers, rows, cols), f32),
            pltpu.VMEM((rows, cols), i32),
            pltpu.VMEM((rows, cols), f32),
            pltpu.VMEM((rows, cols), i32),
            pltpu.VMEM((rows, cols), f32),
            pltpu.VMEM((tracers, cols, rows), f32),
            pltpu.VMEM((cols, rows), f32),
            pltpu.VMEM((cols, half), f32),
            pltpu.VMEM((tracers, 3, cols, half), f32),
            pltpu.VMEM((tracers, rows, cols), f32),
            pltpu.VMEM((rows, cols // 2), f32),
            pltpu.VMEM((2, tracers, REACH, cols), f32),
            pltpu.VMEM((2, tracers, REACH, cols), f32),
            pltpu.VMEM((groups, tracers, group, cols), f32),
            pltpu.VMEM((groups, tracers, group, cols), f32),
            pltpu.SemaphoreType.DMA((5,)),
            pltpu.SemaphoreType.DMA((2,)),
            pltpu.SemaphoreType.DMA((2,)),
            pltpu.SemaphoreType.DMA((groups,)),
            pltpu.SemaphoreType.DMA((groups,)),
        ],
        compiler_params=pltpu.CompilerParams(
            collective_id=0, has_side_effects=True, vmem_limit_bytes=VMEM
        ),
        name="remap_adjoint",
    )(
        cotangent.reshape(tracers, rows, cols),
        lat_cell.reshape(rows, cols),
        lat_frac.reshape(rows, cols),
        lat_end_cell.reshape(1, cols),
        lat_end_frac.reshape(1, cols),
        lon_cell.reshape(rows, cols),
        lon_frac.reshape(rows, cols),
        lon_end_cell.reshape(1, rows),
        lon_end_frac.reshape(1, rows),
    )
    return out.reshape(cotangent.shape)


def solution(mesh):
    whole = P(None, None, "lat", "lon")
    placed = (whole,) + (P(None, "lat", "lon"),) * 8
    body = functools.partial(shards, mesh.shape["lat"], mesh.shape["lon"])
    return jax.shard_map(body, mesh=mesh, in_specs=placed, out_specs=whole, check_vma=False)
```

```python
import functools

import jax
import jax.numpy as jnp
from jax import lax
from jax.experimental import pallas as pl
from jax.experimental.pallas import tpu as pltpu
from jax.sharding import PartitionSpec as P

REACH = 32
GROUP = 128
SEND = 32
VMEM = 63 * 2**20


def take(table, at):
    return jnp.take_along_axis(table, at, axis=1, mode="promise_in_bounds")


def lanes_of(rows, half):
    return lax.broadcasted_iota(jnp.int32, (rows, half), 1)


def upper(length):
    before = lax.broadcasted_iota(jnp.int32, (length, length), 0)
    after = lax.broadcasted_iota(jnp.int32, (length, length), 1)
    return jnp.where(before < after, 1.0, 0.0).astype(jnp.bfloat16)


def running(edges, end, values, tri):
    rows, half = edges[0].shape
    lane = lanes_of(rows, half)
    back = [pltpu.roll(edge, half - 1, 1) for edge in edges]
    width = [
        jnp.where(lane == half - 1, back[1], back[0]) - edges[0],
        jnp.where(lane == half - 1, end, back[1]) - edges[1],
    ]
    whole = jnp.concatenate(
        [jnp.concatenate([v[0] * width[0], v[1] * width[1]], axis=1) for v in values], axis=0
    )
    high = whole.astype(jnp.bfloat16)
    low = (whole - high.astype(jnp.float32)).astype(jnp.bfloat16)
    both = jnp.dot(jnp.concatenate([high, low], axis=0), tri, preferred_element_type=jnp.float32)
    count = whole.shape[0]
    total = both[:count] + both[count:]
    return [
        tuple(
            total[t * rows : (t + 1) * rows, h * half : (h + 1) * half] - values[t][h] * edges[h]
            for h in (0, 1)
        )
        for t in range(len(values))
    ]


def spread(table, lane, shape):
    return jnp.broadcast_to(table[:, lane : lane + 1], shape)


def integral(points, halves, edges, marks, end, values, starts):
    shape = edges[0].shape
    half = shape[1]
    x = jnp.minimum(jnp.maximum(points, marks[0][0]), end)
    if len(halves) == 2:
        upper_half = marks[1][0] <= x

    def pick(pair):
        if len(halves) == 1:
            return pair[halves[0]]
        return jnp.where(upper_half, pair[1], pair[0])

    def fetch(pair, at):
        if len(halves) == 1:
            return take(pair[halves[0]], at)
        return jnp.where(upper_half, take(pair[1], at), take(pair[0], at))

    step = half // 2
    at = jnp.where(pick((marks[0][1], marks[1][1])) <= x, step, 0)
    step //= 2
    while step:
        further = at + step
        at = jnp.where(fetch(edges, further) <= x, further, at)
        step //= 2
    return [fetch(s, at) + fetch(v, at) * x for s, v in zip(starts, values)]


def near_integral(points, reach, source, edges, first, end, values, starts):
    half = edges[0].shape[1]
    length = 2 * half
    x = jnp.minimum(jnp.maximum(points.astype(jnp.float32), first), end)

    def fetch(pair, at):
        lane = jnp.bitwise_and(at, half - 1)
        if source is not None:
            return take(pair, lane)
        return jnp.where(at >= half, take(pair[1], lane), take(pair[0], lane))

    at = points - reach
    step = reach
    while step:
        further = at + step
        found = fetch(edges if source is None else source[0], further)
        ahead = jnp.logical_and(further < length, jnp.logical_or(further < 0, found <= x))
        at = jnp.where(ahead, further, at)
        step //= 2
    at = jnp.clip(at, 0, length - 1)
    tables = zip(starts, values) if source is None else zip(source[1], source[2])
    return [fetch(s, at) + fetch(v, at) * x for s, v in tables]


def step_up(now, before):
    lane = lanes_of(*now.shape)
    return now - jnp.where(lane == 0, before if before is None else pltpu.roll(before, 1, 1), pltpu.roll(now, 1, 1))


MESH = pl.DeviceIdType.MESH


def lat_first(cot_ref, cell_ref, frac_ref, endc_ref, endf_ref, up_ref, down_ref, vt, st, et, endt, mt):
    tracers, lat_rows, cols = cot_ref.shape
    half = lat_rows // 2
    reach = up_ref.shape[1]
    first_cell = lax.axis_index("lat") * lat_rows
    edges = (cell_ref[...] - first_cell).astype(jnp.float32) + frac_ref[...]
    et[...] = edges.T
    end = (endc_ref[...] - first_cell).astype(jnp.float32) + endf_ref[...]
    endt[...] = jnp.broadcast_to(end, (half, cols)).T
    for t in range(tracers):
        vt[t] = cot_ref[t].T
    tri = upper(lat_rows)
    group = min(GROUP, cols)

    @pl.loop(0, cols // group)
    def _(g):
        at = pl.ds(pl.multiple_of(g * group, group), group)
        pair = (et[at, :half], et[at, half:])
        last = endt[at, :]
        values = [(vt[t, at, :half], vt[t, at, half:]) for t in range(tracers)]
        sums = running(pair, last, values, tri)
        lane = lanes_of(group, half)
        first = spread(pair[0], 0, pair[0].shape)
        rim = jnp.where(lane < half // 2, lane + 2 * half, lane - half + 1)

        def ends(both):
            return jnp.where(lane < half // 2, both[0], both[1])

        source = (ends(pair), [ends(s) for s in sums], [ends(v) for v in values])
        got = [
            near_integral(p, reach, src, pair, first, last, values, sums)
            for p, src in ((rim, source), (lane + 1, None))
        ]
        for t in range(tracers):
            st[t, at, :half], st[t, at, half:] = sums[t]
            mt[t, 0, at, :] = step_up(got[0][t], got[0][t])
            mt[t, 1, at, :] = step_up(got[1][t], got[0][t])
            mt[t, 2, at, :] = got[1][t]

    for t in range(tracers):
        halo = mt[t, 0].T
        up_ref[t] = halo[1 : reach + 1]
        down_ref[t] = halo[half - reach :]


def lat_second(reach, mid_ref, vt, st, et, endt, mt):
    tracers, cols, lat_rows = vt.shape
    half = lat_rows // 2
    group = min(GROUP, cols)

    @pl.loop(0, cols // group)
    def _(g):
        at = pl.ds(pl.multiple_of(g * group, group), group)
        pair = (et[at, :half], et[at, half:])
        values = [(vt[t, at, :half], vt[t, at, half:]) for t in range(tracers)]
        starts = [(st[t, at, :half], st[t, at, half:]) for t in range(tracers)]
        first = spread(pair[0], 0, pair[0].shape)
        points = lanes_of(group, half) + (half + 1)
        got = near_integral(points, reach, None, pair, first, endt[at, :], values, starts)
        for t in range(tracers):
            mt[t, 2, at, :] = step_up(got[t], mt[t, 2, at, :])

    for t in range(tracers):
        mid_ref[t, half:] = mt[t, 2].T


def lon_group(at, first_cell, mid_ref, cell_ref, frac_ref, end_ref, own_ref, low_ref, g, tri):
    tracers, rows, cols = mid_ref.shape
    half = cols // 2
    group = low_ref.shape[2]
    edges = (cell_ref[at, :] - first_cell).astype(jnp.float32) + frac_ref[at, :]
    pair = (edges[:, :half], edges[:, half:])
    last = end_ref[at, :]
    values = [(mid_ref[t, at, :half], mid_ref[t, at, half:]) for t in range(tracers)]
    sums = running(pair, last, values, tri)
    lane = lanes_of(group, half)
    halves = ((0,), (0, 1), (0, 1), (1,))
    marks = [[spread(edge, at, edge.shape) for at in (0, half // 2)] for edge in pair]
    got = [
        integral((lane + ((b - 2) * half + 1)).astype(jnp.float32), halves[b], pair, marks, last, values, sums)
        for b in range(4)
    ]
    none = jnp.zeros((group, half), jnp.float32)
    for t in range(tracers):
        for b in range(4):
            cells = step_up(got[b][t], got[b - 1][t] if b else none)
            start = (b % 2) * half
            if b < 2:
                low_ref[g, t, :, start : start + half] = cells
            else:
                own_ref[t, at, start : start + half] = cells


def kernel(
    lats, lons, cot_hbm, latc_hbm, latf_hbm, lat_endc, lat_endf, lonc_hbm, lonf_hbm, lon_endc, lon_endf,
    out_ref, cot, latc, latf, lonc, lonf, vt, st, et, endt, mt, mid, lon_end, edge_out, edge_in, low_out, low_in,
    load_sem, edge_send, edge_recv, low_send, low_recv,
):
    tracers, rows, cols = cot.shape
    half = rows // 2
    reach = edge_out.shape[2]
    groups, _, group, _ = low_out.shape
    loads = [
        pltpu.make_async_copy(source, target, load_sem.at[k])
        for k, (source, target) in enumerate(
            zip((latc_hbm, latf_hbm, cot_hbm, lonc_hbm, lonf_hbm), (latc, latf, cot, lonc, lonf))
        )
    ]
    for load in loads:
        load.start()
    la, lo = lax.axis_index("lat"), lax.axis_index("lon")
    has_up, has_down = la < lats - 1, la > 0
    has_right, has_left = lo < lons - 1, lo > 0
    barrier = pltpu.get_barrier_semaphore()
    for there, where in (
        (has_up, {"lat": la + 1}),
        (has_down, {"lat": la - 1}),
        (has_right, {"lon": lo + 1}),
        (has_left, {"lon": lo - 1}),
    ):

        @pl.when(there)
        def _(where=where):
            pl.semaphore_signal(barrier, inc=1, device_id=where, device_id_type=MESH)

    end = (lon_endc[...] - lo * cols).astype(jnp.float32) + lon_endf[...]
    lon_end[...] = jnp.broadcast_to(end, (cols // 2, rows)).T
    for load in loads:
        load.wait()
    lat_first(cot, latc, latf, lat_endc, lat_endf, edge_out.at[0], edge_out.at[1], vt, st, et, endt, mt)
    peers = [there.astype(jnp.int32) for there in (has_up, has_down, has_right, has_left)]
    pl.semaphore_wait(barrier, peers[0] + peers[1] + peers[2] + peers[3])

    def edge(k, where):
        return pltpu.make_async_remote_copy(
            src_ref=edge_out.at[k],
            dst_ref=edge_in.at[k],
            send_sem=edge_send.at[k],
            recv_sem=edge_recv.at[k],
            device_id={"lat": where},
            device_id_type=MESH,
        )

    up, down = edge(0, la + 1), edge(1, la - 1)
    pl.when(has_up)(up.start)
    pl.when(has_down)(down.start)
    for t in range(tracers):
        mid[t, :half] = mt[t, 1].T

    def low(g):
        return pltpu.make_async_remote_copy(
            src_ref=low_out.at[g],
            dst_ref=low_in.at[g],
            send_sem=low_send.at[g],
            recv_sem=low_recv.at[g],
            device_id={"lon": lo - 1},
            device_id_type=MESH,
        )

    tri = upper(cols)

    @pl.loop(0, groups)
    def _(k):
        @pl.when(k == max(groups // 2 - 1, 0))
        def _():
            lat_second(reach, mid, vt, st, et, endt, mt)

        @pl.when(k == max(groups - 2, 0))
        def _():
            @pl.when(has_down)
            def _():
                up.wait_recv()
                mid[:, :reach] += edge_in[0]

            @pl.when(has_up)
            def _():
                down.wait_recv()
                mid[:, rows - reach :] += edge_in[1]

        g = lax.rem(k + 1, groups)
        at = pl.ds(pl.multiple_of(g * group, group), group)
        lon_group(at, lo * cols, mid, lonc, lonf, lon_end, out_ref, low_out, g, tri)
        pl.when(has_left)(low(g).start)

    @pl.when(has_right)
    def _():
        @pl.loop(0, groups)
        def _(k):
            g = lax.rem(k + 1, groups)
            low(g).wait_recv()
            at = pl.ds(pl.multiple_of(g * group, group), group)
            out_ref[:, at, :] += low_in[g]

    pl.when(has_up)(up.wait_send)
    pl.when(has_down)(down.wait_send)

    @pl.when(has_left)
    def _():
        @pl.loop(0, groups)
        def _(g):
            low(g).wait_send()


def shards(lats, lons, cotangent, lat_cell, lat_frac, lat_end_cell, lat_end_frac, lon_cell, lon_frac, lon_end_cell, lon_end_frac):
    tracers, levels, rows, cols = cotangent.shape
    f32, i32 = jnp.float32, jnp.int32
    half = rows // 2
    group = min(SEND, rows)
    groups = rows // group
    anywhere, vmem = pl.BlockSpec(memory_space=pl.ANY), pl.BlockSpec(memory_space=pltpu.VMEM)
    out = pl.pallas_call(
        functools.partial(kernel, lats, lons),
        out_shape=jax.ShapeDtypeStruct((tracers, rows, cols), f32),
        in_specs=[anywhere, anywhere, anywhere, vmem, vmem, anywhere, anywhere, vmem, vmem],
        out_specs=vmem,
        scratch_shapes=[
            pltpu.VMEM((tracers, rows, cols), f32),
            pltpu.VMEM((rows, cols), i32),
            pltpu.VMEM((rows, cols), f32),
            pltpu.VMEM((rows, cols), i32),
            pltpu.VMEM((rows, cols), f32),
            pltpu.VMEM((tracers, cols, rows), f32),
            pltpu.VMEM((tracers, cols, rows), f32),
            pltpu.VMEM((cols, rows), f32),
            pltpu.VMEM((cols, half), f32),
            pltpu.VMEM((tracers, 3, cols, half), f32),
            pltpu.VMEM((tracers, rows, cols), f32),
            pltpu.VMEM((rows, cols // 2), f32),
            pltpu.VMEM((2, tracers, REACH, cols), f32),
            pltpu.VMEM((2, tracers, REACH, cols), f32),
            pltpu.VMEM((groups, tracers, group, cols), f32),
            pltpu.VMEM((groups, tracers, group, cols), f32),
            pltpu.SemaphoreType.DMA((5,)),
            pltpu.SemaphoreType.DMA((2,)),
            pltpu.SemaphoreType.DMA((2,)),
            pltpu.SemaphoreType.DMA((groups,)),
            pltpu.SemaphoreType.DMA((groups,)),
        ],
        compiler_params=pltpu.CompilerParams(
            collective_id=0, has_side_effects=True, vmem_limit_bytes=VMEM
        ),
        name="remap_adjoint",
    )(
        cotangent.reshape(tracers, rows, cols),
        lat_cell.reshape(rows, cols),
        lat_frac.reshape(rows, cols),
        lat_end_cell.reshape(1, cols),
        lat_end_frac.reshape(1, cols),
        lon_cell.reshape(rows, cols),
        lon_frac.reshape(rows, cols),
        lon_end_cell.reshape(1, rows),
        lon_end_frac.reshape(1, rows),
    )
    return out.reshape(cotangent.shape)


def solution(mesh):
    whole = P(None, None, "lat", "lon")
    placed = (whole,) + (P(None, "lat", "lon"),) * 8
    body = functools.partial(shards, mesh.shape["lat"], mesh.shape["lon"])
    return jax.shard_map(body, mesh=mesh, in_specs=placed, out_specs=whole, check_vma=False)
```

```python
import functools

import jax
import jax.numpy as jnp
from jax import lax
from jax.experimental import pallas as pl
from jax.experimental.pallas import tpu as pltpu
from jax.sharding import PartitionSpec as P

REACH = 32
GROUP = 128
SEND = 32
VMEM = 63 * 2**20


def take(table, at):
    return jnp.take_along_axis(table, at, axis=1, mode="promise_in_bounds")


def lanes_of(rows, half):
    return lax.broadcasted_iota(jnp.int32, (rows, half), 1)


def upper(length):
    before = lax.broadcasted_iota(jnp.int32, (length, length), 0)
    after = lax.broadcasted_iota(jnp.int32, (length, length), 1)
    return jnp.where(before < after, 1.0, 0.0).astype(jnp.bfloat16)


def running(edges, end, values, tri):
    rows, half = edges[0].shape
    lane = lanes_of(rows, half)
    back = [pltpu.roll(edge, half - 1, 1) for edge in edges]
    width = [
        jnp.where(lane == half - 1, back[1], back[0]) - edges[0],
        jnp.where(lane == half - 1, end, back[1]) - edges[1],
    ]
    whole = jnp.concatenate(
        [jnp.concatenate([v[0] * width[0], v[1] * width[1]], axis=1) for v in values], axis=0
    )
    high = whole.astype(jnp.bfloat16)
    low = (whole - high.astype(jnp.float32)).astype(jnp.bfloat16)
    both = jnp.dot(jnp.concatenate([high, low], axis=0), tri, preferred_element_type=jnp.float32)
    count = whole.shape[0]
    total = both[:count] + both[count:]
    return [
        tuple(
            total[t * rows : (t + 1) * rows, h * half : (h + 1) * half] - values[t][h] * edges[h]
            for h in (0, 1)
        )
        for t in range(len(values))
    ]


def spread(table, lane, shape):
    return jnp.broadcast_to(table[:, lane : lane + 1], shape)


def integral(points, halves, edges, marks, end, values, starts):
    shape = edges[0].shape
    half = shape[1]
    x = jnp.minimum(jnp.maximum(points, marks[0][0]), end)
    if len(halves) == 2:
        upper_half = marks[1][0] <= x

    def pick(pair):
        if len(halves) == 1:
            return pair[halves[0]]
        return jnp.where(upper_half, pair[1], pair[0])

    def fetch(pair, at):
        if len(halves) == 1:
            return take(pair[halves[0]], at)
        return jnp.where(upper_half, take(pair[1], at), take(pair[0], at))

    step = half // 2
    beyond = pick((marks[0][2], marks[1][2])) <= x
    step //= 2
    middle = pick([jnp.where(beyond, mark[3], mark[1]) for mark in marks])
    at = jnp.where(beyond, 2 * step, 0) + jnp.where(middle <= x, step, 0)
    step //= 2
    while step:
        further = at + step
        at = jnp.where(fetch(edges, further) <= x, further, at)
        step //= 2
    return [fetch(s, at) + fetch(v, at) * x for s, v in zip(starts, values)]


def near_integral(points, reach, source, edges, first, end, values, starts):
    half = edges[0].shape[1]
    length = 2 * half
    x = jnp.minimum(jnp.maximum(points.astype(jnp.float32), first), end)

    def fetch(pair, at):
        lane = jnp.bitwise_and(at, half - 1)
        if source is not None:
            return take(pair, lane)
        return jnp.where(at >= half, take(pair[1], lane), take(pair[0], lane))

    at = points - reach
    step = reach
    while step:
        further = at + step
        found = fetch(edges if source is None else source[0], further)
        ahead = jnp.logical_and(further < length, jnp.logical_or(further < 0, found <= x))
        at = jnp.where(ahead, further, at)
        step //= 2
    at = jnp.clip(at, 0, length - 1)
    tables = zip(starts, values) if source is None else zip(source[1], source[2])
    return [fetch(s, at) + fetch(v, at) * x for s, v in tables]


def step_up(now, before):
    lane = lanes_of(*now.shape)
    return now - jnp.where(lane == 0, before if before is None else pltpu.roll(before, 1, 1), pltpu.roll(now, 1, 1))


MESH = pl.DeviceIdType.MESH


def lat_first(wait, cot_ref, cell_ref, frac_ref, endc_ref, endf_ref, up_ref, down_ref, vt, st, et, endt, mt):
    tracers, lat_rows, cols = cot_ref.shape
    half = lat_rows // 2
    reach = up_ref.shape[1]
    first_cell = lax.axis_index("lat") * lat_rows
    edges = (cell_ref[...] - first_cell).astype(jnp.float32) + frac_ref[...]
    et[...] = edges.T
    end = (endc_ref[...] - first_cell).astype(jnp.float32) + endf_ref[...]
    endt[...] = jnp.broadcast_to(end, (half, cols)).T
    wait()
    for t in range(tracers):
        vt[t] = cot_ref[t].T
    tri = upper(lat_rows)
    group = min(GROUP, cols)

    @pl.loop(0, cols // group)
    def _(g):
        at = pl.ds(pl.multiple_of(g * group, group), group)
        pair = (et[at, :half], et[at, half:])
        last = endt[at, :]
        values = [(vt[t, at, :half], vt[t, at, half:]) for t in range(tracers)]
        sums = running(pair, last, values, tri)
        lane = lanes_of(group, half)
        first = spread(pair[0], 0, pair[0].shape)
        rim = jnp.where(lane < half // 2, lane + 2 * half, lane - half + 1)

        def ends(both):
            return jnp.where(lane < half // 2, both[0], both[1])

        source = (ends(pair), [ends(s) for s in sums], [ends(v) for v in values])
        got = [
            near_integral(p, reach, src, pair, first, last, values, sums)
            for p, src in ((rim, source), (lane + 1, None))
        ]
        for t in range(tracers):
            st[t, at, :half], st[t, at, half:] = sums[t]
            mt[t, 0, at, :] = step_up(got[0][t], got[0][t])
            mt[t, 1, at, :] = step_up(got[1][t], got[0][t])
            mt[t, 2, at, :] = got[1][t]

    for t in range(tracers):
        halo = mt[t, 0].T
        up_ref[t] = halo[1 : reach + 1]
        down_ref[t] = halo[half - reach :]


def lat_second(reach, mid_ref, vt, st, et, endt, mt):
    tracers, cols, lat_rows = vt.shape
    half = lat_rows // 2
    group = min(GROUP, cols)

    @pl.loop(0, cols // group)
    def _(g):
        at = pl.ds(pl.multiple_of(g * group, group), group)
        pair = (et[at, :half], et[at, half:])
        values = [(vt[t, at, :half], vt[t, at, half:]) for t in range(tracers)]
        starts = [(st[t, at, :half], st[t, at, half:]) for t in range(tracers)]
        first = spread(pair[0], 0, pair[0].shape)
        points = lanes_of(group, half) + (half + 1)
        got = near_integral(points, reach, None, pair, first, endt[at, :], values, starts)
        for t in range(tracers):
            mt[t, 2, at, :] = step_up(got[t], mt[t, 2, at, :])

    for t in range(tracers):
        mid_ref[t, half:] = mt[t, 2].T


def lon_group(at, first_cell, mid_ref, cell_ref, frac_ref, end_ref, own_ref, low_ref, g, tri):
    tracers, rows, cols = mid_ref.shape
    half = cols // 2
    group = low_ref.shape[2]
    edges = (cell_ref[at, :] - first_cell).astype(jnp.float32) + frac_ref[at, :]
    pair = (edges[:, :half], edges[:, half:])
    last = end_ref[at, :]
    values = [(mid_ref[t, at, :half], mid_ref[t, at, half:]) for t in range(tracers)]
    sums = running(pair, last, values, tri)
    lane = lanes_of(group, half)
    halves = ((0,), (0, 1), (0, 1), (1,))
    marks = [[spread(edge, at, edge.shape) for at in (0, half // 4, half // 2, 3 * (half // 4))] for edge in pair]
    got = [
        integral((lane + ((b - 2) * half + 1)).astype(jnp.float32), halves[b], pair, marks, last, values, sums)
        for b in range(4)
    ]
    none = jnp.zeros((group, half), jnp.float32)
    for t in range(tracers):
        for b in range(4):
            cells = step_up(got[b][t], got[b - 1][t] if b else none)
            start = (b % 2) * half
            if b < 2:
                low_ref[g, t, :, start : start + half] = cells
            else:
                own_ref[t, at, start : start + half] = cells


def kernel(
    lats, lons, cot_hbm, latc_hbm, latf_hbm, lat_endc, lat_endf, lonc_hbm, lonf_hbm, lon_endc, lon_endf,
    out_ref, cot, latc, latf, lonc, lonf, vt, st, et, endt, mt, mid, lon_end, edge_out, edge_in, low_out, low_in,
    load_sem, edge_send, edge_recv, low_send, low_recv,
):
    tracers, rows, cols = cot.shape
    half = rows // 2
    reach = edge_out.shape[2]
    groups, _, group, _ = low_out.shape
    loads = [
        pltpu.make_async_copy(source, target, load_sem.at[k])
        for k, (source, target) in enumerate(
            zip((latc_hbm, latf_hbm, cot_hbm, lonc_hbm, lonf_hbm), (latc, latf, cot, lonc, lonf))
        )
    ]
    for load in loads:
        load.start()
    la, lo = lax.axis_index("lat"), lax.axis_index("lon")
    has_up, has_down = la < lats - 1, la > 0
    has_right, has_left = lo < lons - 1, lo > 0
    barrier = pltpu.get_barrier_semaphore()
    for there, where in (
        (has_up, {"lat": la + 1}),
        (has_down, {"lat": la - 1}),
        (has_right, {"lon": lo + 1}),
        (has_left, {"lon": lo - 1}),
    ):

        @pl.when(there)
        def _(where=where):
            pl.semaphore_signal(barrier, inc=1, device_id=where, device_id_type=MESH)

    end = (lon_endc[...] - lo * cols).astype(jnp.float32) + lon_endf[...]
    lon_end[...] = jnp.broadcast_to(end, (cols // 2, rows)).T
    loads[0].wait()
    loads[1].wait()
    lat_first(loads[2].wait, cot, latc, latf, lat_endc, lat_endf, edge_out.at[0], edge_out.at[1], vt, st, et, endt, mt)
    peers = [there.astype(jnp.int32) for there in (has_up, has_down, has_right, has_left)]
    pl.semaphore_wait(barrier, peers[0] + peers[1] + peers[2] + peers[3])

    def edge(k, where):
        return pltpu.make_async_remote_copy(
            src_ref=edge_out.at[k],
            dst_ref=edge_in.at[k],
            send_sem=edge_send.at[k],
            recv_sem=edge_recv.at[k],
            device_id={"lat": where},
            device_id_type=MESH,
        )

    up, down = edge(0, la + 1), edge(1, la - 1)
    pl.when(has_up)(up.start)
    pl.when(has_down)(down.start)
    for t in range(tracers):
        mid[t, :half] = mt[t, 1].T

    def low(g):
        return pltpu.make_async_remote_copy(
            src_ref=low_out.at[g],
            dst_ref=low_in.at[g],
            send_sem=low_send.at[g],
            recv_sem=low_recv.at[g],
            device_id={"lon": lo - 1},
            device_id_type=MESH,
        )

    tri = upper(cols)
    loads[3].wait()
    loads[4].wait()

    @pl.loop(0, groups)
    def _(k):
        @pl.when(k == max(groups // 2 - 1, 0))
        def _():
            lat_second(reach, mid, vt, st, et, endt, mt)

        @pl.when(k == max(groups - 2, 0))
        def _():
            @pl.when(has_down)
            def _():
                up.wait_recv()
                mid[:, :reach] += edge_in[0]

            @pl.when(has_up)
            def _():
                down.wait_recv()
                mid[:, rows - reach :] += edge_in[1]

        g = lax.rem(k + 1, groups)
        at = pl.ds(pl.multiple_of(g * group, group), group)
        lon_group(at, lo * cols, mid, lonc, lonf, lon_end, out_ref, low_out, g, tri)
        pl.when(has_left)(low(g).start)

    @pl.when(has_right)
    def _():
        @pl.loop(0, groups)
        def _(k):
            g = lax.rem(k + 1, groups)
            low(g).wait_recv()
            at = pl.ds(pl.multiple_of(g * group, group), group)
            out_ref[:, at, :] += low_in[g]

    pl.when(has_up)(up.wait_send)
    pl.when(has_down)(down.wait_send)

    @pl.when(has_left)
    def _():
        @pl.loop(0, groups)
        def _(g):
            low(g).wait_send()


def shards(lats, lons, cotangent, lat_cell, lat_frac, lat_end_cell, lat_end_frac, lon_cell, lon_frac, lon_end_cell, lon_end_frac):
    tracers, levels, rows, cols = cotangent.shape
    f32, i32 = jnp.float32, jnp.int32
    half = rows // 2
    group = min(SEND, rows)
    groups = rows // group
    anywhere, vmem = pl.BlockSpec(memory_space=pl.ANY), pl.BlockSpec(memory_space=pltpu.VMEM)
    out = pl.pallas_call(
        functools.partial(kernel, lats, lons),
        out_shape=jax.ShapeDtypeStruct((tracers, rows, cols), f32),
        in_specs=[anywhere, anywhere, anywhere, vmem, vmem, anywhere, anywhere, vmem, vmem],
        out_specs=vmem,
        scratch_shapes=[
            pltpu.VMEM((tracers, rows, cols), f32),
            pltpu.VMEM((rows, cols), i32),
            pltpu.VMEM((rows, cols), f32),
            pltpu.VMEM((rows, cols), i32),
            pltpu.VMEM((rows, cols), f32),
            pltpu.VMEM((tracers, cols, rows), f32),
            pltpu.VMEM((tracers, cols, rows), f32),
            pltpu.VMEM((cols, rows), f32),
            pltpu.VMEM((cols, half), f32),
            pltpu.VMEM((tracers, 3, cols, half), f32),
            pltpu.VMEM((tracers, rows, cols), f32),
            pltpu.VMEM((rows, cols // 2), f32),
            pltpu.VMEM((2, tracers, REACH, cols), f32),
            pltpu.VMEM((2, tracers, REACH, cols), f32),
            pltpu.VMEM((groups, tracers, group, cols), f32),
            pltpu.VMEM((groups, tracers, group, cols), f32),
            pltpu.SemaphoreType.DMA((5,)),
            pltpu.SemaphoreType.DMA((2,)),
            pltpu.SemaphoreType.DMA((2,)),
            pltpu.SemaphoreType.DMA((groups,)),
            pltpu.SemaphoreType.DMA((groups,)),
        ],
        compiler_params=pltpu.CompilerParams(
            collective_id=0, has_side_effects=True, vmem_limit_bytes=VMEM
        ),
        name="remap_adjoint",
    )(
        cotangent.reshape(tracers, rows, cols),
        lat_cell.reshape(rows, cols),
        lat_frac.reshape(rows, cols),
        lat_end_cell.reshape(1, cols),
        lat_end_frac.reshape(1, cols),
        lon_cell.reshape(rows, cols),
        lon_frac.reshape(rows, cols),
        lon_end_cell.reshape(1, rows),
        lon_end_frac.reshape(1, rows),
    )
    return out.reshape(cotangent.shape)


def solution(mesh):
    whole = P(None, None, "lat", "lon")
    placed = (whole,) + (P(None, "lat", "lon"),) * 8
    body = functools.partial(shards, mesh.shape["lat"], mesh.shape["lon"])
    return jax.shard_map(body, mesh=mesh, in_specs=placed, out_specs=whole, check_vma=False)
```

```python
import functools

import jax
import jax.numpy as jnp
from jax import lax
from jax.experimental import pallas as pl
from jax.experimental.pallas import tpu as pltpu
from jax.sharding import PartitionSpec as P

REACH = 32
GROUP = 256
SEND = 32
VMEM = 63 * 2**20


def take(table, at):
    return jnp.take_along_axis(table, at, axis=1, mode="promise_in_bounds")


def lanes_of(rows, half):
    return lax.broadcasted_iota(jnp.int32, (rows, half), 1)


def upper(length):
    before = lax.broadcasted_iota(jnp.int32, (length, length), 0)
    after = lax.broadcasted_iota(jnp.int32, (length, length), 1)
    return jnp.where(before < after, 1.0, 0.0).astype(jnp.bfloat16)


def running(edges, end, values, tri):
    rows, half = edges[0].shape
    lane = lanes_of(rows, half)
    back = [pltpu.roll(edge, half - 1, 1) for edge in edges]
    width = [
        jnp.where(lane == half - 1, back[1], back[0]) - edges[0],
        jnp.where(lane == half - 1, end, back[1]) - edges[1],
    ]
    whole = jnp.concatenate(
        [jnp.concatenate([v[0] * width[0], v[1] * width[1]], axis=1) for v in values], axis=0
    )
    high = whole.astype(jnp.bfloat16)
    low = (whole - high.astype(jnp.float32)).astype(jnp.bfloat16)
    both = jnp.dot(jnp.concatenate([high, low], axis=0), tri, preferred_element_type=jnp.float32)
    count = whole.shape[0]
    total = both[:count] + both[count:]
    return [
        tuple(
            total[t * rows : (t + 1) * rows, h * half : (h + 1) * half] - values[t][h] * edges[h]
            for h in (0, 1)
        )
        for t in range(len(values))
    ]


def spread(table, lane, shape):
    return jnp.broadcast_to(table[:, lane : lane + 1], shape)


def integral(points, halves, edges, marks, end, values, starts):
    shape = edges[0].shape
    half = shape[1]
    x = jnp.minimum(jnp.maximum(points, marks[0][0]), end)
    if len(halves) == 2:
        upper_half = marks[1][0] <= x

    def pick(pair):
        if len(halves) == 1:
            return pair[halves[0]]
        return jnp.where(upper_half, pair[1], pair[0])

    def fetch(pair, at):
        if len(halves) == 1:
            return take(pair[halves[0]], at)
        return jnp.where(upper_half, take(pair[1], at), take(pair[0], at))

    step = half // 2
    beyond = pick((marks[0][2], marks[1][2])) <= x
    step //= 2
    middle = pick([jnp.where(beyond, mark[3], mark[1]) for mark in marks])
    at = jnp.where(beyond, 2 * step, 0) + jnp.where(middle <= x, step, 0)
    step //= 2
    while step:
        further = at + step
        at = jnp.where(fetch(edges, further) <= x, further, at)
        step //= 2
    return [fetch(s, at) + fetch(v, at) * x for s, v in zip(starts, values)]


def near_integral(points, reach, source, edges, first, end, values, starts):
    half = edges[0].shape[1]
    length = 2 * half
    x = jnp.minimum(jnp.maximum(points.astype(jnp.float32), first), end)

    def fetch(pair, at):
        lane = jnp.bitwise_and(at, half - 1)
        if source is not None:
            return take(pair, lane)
        return jnp.where(at >= half, take(pair[1], lane), take(pair[0], lane))

    at = points - reach
    step = reach
    while step:
        further = at + step
        found = fetch(edges if source is None else source[0], further)
        ahead = jnp.logical_and(further < length, jnp.logical_or(further < 0, found <= x))
        at = jnp.where(ahead, further, at)
        step //= 2
    at = jnp.clip(at, 0, length - 1)
    tables = zip(starts, values) if source is None else zip(source[1], source[2])
    return [fetch(s, at) + fetch(v, at) * x for s, v in tables]


def step_up(now, before):
    lane = lanes_of(*now.shape)
    return now - jnp.where(lane == 0, before if before is None else pltpu.roll(before, 1, 1), pltpu.roll(now, 1, 1))


MESH = pl.DeviceIdType.MESH


def lat_first(wait, cot_ref, cell_ref, frac_ref, endc_ref, endf_ref, up_ref, down_ref, vt, st, et, endt, mt):
    tracers, lat_rows, cols = cot_ref.shape
    half = lat_rows // 2
    reach = up_ref.shape[1]
    first_cell = lax.axis_index("lat") * lat_rows
    edges = (cell_ref[...] - first_cell).astype(jnp.float32) + frac_ref[...]
    et[...] = edges.T
    end = (endc_ref[...] - first_cell).astype(jnp.float32) + endf_ref[...]
    endt[...] = jnp.broadcast_to(end, (half, cols)).T
    wait()
    for t in range(tracers):
        vt[t] = cot_ref[t].T
    tri = upper(lat_rows)
    group = min(GROUP, cols)

    @pl.loop(0, cols // group)
    def _(g):
        at = pl.ds(pl.multiple_of(g * group, group), group)
        pair = (et[at, :half], et[at, half:])
        last = endt[at, :]
        values = [(vt[t, at, :half], vt[t, at, half:]) for t in range(tracers)]
        sums = running(pair, last, values, tri)
        lane = lanes_of(group, half)
        first = spread(pair[0], 0, pair[0].shape)
        rim = jnp.where(lane < half // 2, lane + 2 * half, lane - half + 1)

        def ends(both):
            return jnp.where(lane < half // 2, both[0], both[1])

        source = (ends(pair), [ends(s) for s in sums], [ends(v) for v in values])
        got = [
            near_integral(p, reach, src, pair, first, last, values, sums)
            for p, src in ((rim, source), (lane + 1, None))
        ]
        for t in range(tracers):
            st[t, at, :half], st[t, at, half:] = sums[t]
            mt[t, 0, at, :] = step_up(got[0][t], got[0][t])
            mt[t, 1, at, :] = step_up(got[1][t], got[0][t])
            mt[t, 2, at, :] = got[1][t]

    for t in range(tracers):
        halo = mt[t, 0].T
        up_ref[t] = halo[1 : reach + 1]
        down_ref[t] = halo[half - reach :]


def lat_second(reach, mid_ref, vt, st, et, endt, mt):
    tracers, cols, lat_rows = vt.shape
    half = lat_rows // 2
    group = min(GROUP, cols)

    @pl.loop(0, cols // group)
    def _(g):
        at = pl.ds(pl.multiple_of(g * group, group), group)
        pair = (et[at, :half], et[at, half:])
        values = [(vt[t, at, :half], vt[t, at, half:]) for t in range(tracers)]
        starts = [(st[t, at, :half], st[t, at, half:]) for t in range(tracers)]
        first = spread(pair[0], 0, pair[0].shape)
        points = lanes_of(group, half) + (half + 1)
        got = near_integral(points, reach, None, pair, first, endt[at, :], values, starts)
        for t in range(tracers):
            mt[t, 2, at, :] = step_up(got[t], mt[t, 2, at, :])

    for t in range(tracers):
        mid_ref[t, half:] = mt[t, 2].T


def lon_group(at, first_cell, mid_ref, cell_ref, frac_ref, end_ref, own_ref, low_ref, g, tri):
    tracers, rows, cols = mid_ref.shape
    half = cols // 2
    group = low_ref.shape[2]
    edges = (cell_ref[at, :] - first_cell).astype(jnp.float32) + frac_ref[at, :]
    pair = (edges[:, :half], edges[:, half:])
    last = end_ref[at, :]
    values = [(mid_ref[t, at, :half], mid_ref[t, at, half:]) for t in range(tracers)]
    sums = running(pair, last, values, tri)
    lane = lanes_of(group, half)
    halves = ((0,), (0, 1), (0, 1), (1,))
    marks = [[spread(edge, at, edge.shape) for at in (0, half // 4, half // 2, 3 * (half // 4))] for edge in pair]
    got = [
        integral((lane + ((b - 2) * half + 1)).astype(jnp.float32), halves[b], pair, marks, last, values, sums)
        for b in range(4)
    ]
    none = jnp.zeros((group, half), jnp.float32)
    for t in range(tracers):
        for b in range(4):
            cells = step_up(got[b][t], got[b - 1][t] if b else none)
            start = (b % 2) * half
            if b < 2:
                low_ref[g, t, :, start : start + half] = cells
            else:
                own_ref[t, at, start : start + half] = cells


def kernel(
    lats, lons, cot_hbm, latc_hbm, latf_hbm, lat_endc, lat_endf, lonc_hbm, lonf_hbm, lon_endc, lon_endf,
    out_ref, cot, latc, latf, lonc, lonf, vt, st, et, endt, mt, mid, lon_end, edge_out, edge_in, low_out, low_in,
    load_sem, edge_send, edge_recv, low_send, low_recv,
):
    tracers, rows, cols = cot.shape
    half = rows // 2
    reach = edge_out.shape[2]
    groups, _, group, _ = low_out.shape
    loads = [
        pltpu.make_async_copy(source, target, load_sem.at[k])
        for k, (source, target) in enumerate(
            zip((latc_hbm, latf_hbm, cot_hbm, lonc_hbm, lonf_hbm), (latc, latf, cot, lonc, lonf))
        )
    ]
    for load in loads:
        load.start()
    la, lo = lax.axis_index("lat"), lax.axis_index("lon")
    has_up, has_down = la < lats - 1, la > 0
    has_right, has_left = lo < lons - 1, lo > 0
    barrier = pltpu.get_barrier_semaphore()
    for there, where in (
        (has_up, {"lat": la + 1}),
        (has_down, {"lat": la - 1}),
        (has_right, {"lon": lo + 1}),
        (has_left, {"lon": lo - 1}),
    ):

        @pl.when(there)
        def _(where=where):
            pl.semaphore_signal(barrier, inc=1, device_id=where, device_id_type=MESH)

    end = (lon_endc[...] - lo * cols).astype(jnp.float32) + lon_endf[...]
    lon_end[...] = jnp.broadcast_to(end, (cols // 2, rows)).T
    loads[0].wait()
    loads[1].wait()
    lat_first(loads[2].wait, cot, latc, latf, lat_endc, lat_endf, edge_out.at[0], edge_out.at[1], vt, st, et, endt, mt)
    peers = [there.astype(jnp.int32) for there in (has_up, has_down, has_right, has_left)]
    pl.semaphore_wait(barrier, peers[0] + peers[1] + peers[2] + peers[3])

    def edge(k, where):
        return pltpu.make_async_remote_copy(
            src_ref=edge_out.at[k],
            dst_ref=edge_in.at[k],
            send_sem=edge_send.at[k],
            recv_sem=edge_recv.at[k],
            device_id={"lat": where},
            device_id_type=MESH,
        )

    up, down = edge(0, la + 1), edge(1, la - 1)
    pl.when(has_up)(up.start)
    pl.when(has_down)(down.start)
    for t in range(tracers):
        mid[t, :half] = mt[t, 1].T

    def low(g):
        return pltpu.make_async_remote_copy(
            src_ref=low_out.at[g],
            dst_ref=low_in.at[g],
            send_sem=low_send.at[g],
            recv_sem=low_recv.at[g],
            device_id={"lon": lo - 1},
            device_id_type=MESH,
        )

    tri = upper(cols)
    loads[3].wait()
    loads[4].wait()

    @pl.loop(0, groups)
    def _(k):
        @pl.when(k == max(groups // 2 - 1, 0))
        def _():
            lat_second(reach, mid, vt, st, et, endt, mt)

        @pl.when(k == max(groups - 2, 0))
        def _():
            @pl.when(has_down)
            def _():
                up.wait_recv()
                mid[:, :reach] += edge_in[0]

            @pl.when(has_up)
            def _():
                down.wait_recv()
                mid[:, rows - reach :] += edge_in[1]

        g = lax.rem(k + 1, groups)
        at = pl.ds(pl.multiple_of(g * group, group), group)
        lon_group(at, lo * cols, mid, lonc, lonf, lon_end, out_ref, low_out, g, tri)
        pl.when(has_left)(low(g).start)

    @pl.when(has_right)
    def _():
        @pl.loop(0, groups)
        def _(k):
            g = lax.rem(k + 1, groups)
            low(g).wait_recv()
            at = pl.ds(pl.multiple_of(g * group, group), group)
            out_ref[:, at, :] += low_in[g]

    pl.when(has_up)(up.wait_send)
    pl.when(has_down)(down.wait_send)

    @pl.when(has_left)
    def _():
        @pl.loop(0, groups)
        def _(g):
            low(g).wait_send()


def shards(lats, lons, cotangent, lat_cell, lat_frac, lat_end_cell, lat_end_frac, lon_cell, lon_frac, lon_end_cell, lon_end_frac):
    tracers, levels, rows, cols = cotangent.shape
    f32, i32 = jnp.float32, jnp.int32
    half = rows // 2
    group = min(SEND, rows)
    groups = rows // group
    anywhere, vmem = pl.BlockSpec(memory_space=pl.ANY), pl.BlockSpec(memory_space=pltpu.VMEM)
    out = pl.pallas_call(
        functools.partial(kernel, lats, lons),
        out_shape=jax.ShapeDtypeStruct((tracers, rows, cols), f32),
        in_specs=[anywhere, anywhere, anywhere, vmem, vmem, anywhere, anywhere, vmem, vmem],
        out_specs=vmem,
        scratch_shapes=[
            pltpu.VMEM((tracers, rows, cols), f32),
            pltpu.VMEM((rows, cols), i32),
            pltpu.VMEM((rows, cols), f32),
            pltpu.VMEM((rows, cols), i32),
            pltpu.VMEM((rows, cols), f32),
            pltpu.VMEM((tracers, cols, rows), f32),
            pltpu.VMEM((tracers, cols, rows), f32),
            pltpu.VMEM((cols, rows), f32),
            pltpu.VMEM((cols, half), f32),
            pltpu.VMEM((tracers, 3, cols, half), f32),
            pltpu.VMEM((tracers, rows, cols), f32),
            pltpu.VMEM((rows, cols // 2), f32),
            pltpu.VMEM((2, tracers, REACH, cols), f32),
            pltpu.VMEM((2, tracers, REACH, cols), f32),
            pltpu.VMEM((groups, tracers, group, cols), f32),
            pltpu.VMEM((groups, tracers, group, cols), f32),
            pltpu.SemaphoreType.DMA((5,)),
            pltpu.SemaphoreType.DMA((2,)),
            pltpu.SemaphoreType.DMA((2,)),
            pltpu.SemaphoreType.DMA((groups,)),
            pltpu.SemaphoreType.DMA((groups,)),
        ],
        compiler_params=pltpu.CompilerParams(
            collective_id=0, has_side_effects=True, vmem_limit_bytes=VMEM
        ),
        name="remap_adjoint",
    )(
        cotangent.reshape(tracers, rows, cols),
        lat_cell.reshape(rows, cols),
        lat_frac.reshape(rows, cols),
        lat_end_cell.reshape(1, cols),
        lat_end_frac.reshape(1, cols),
        lon_cell.reshape(rows, cols),
        lon_frac.reshape(rows, cols),
        lon_end_cell.reshape(1, rows),
        lon_end_frac.reshape(1, rows),
    )
    return out.reshape(cotangent.shape)


def solution(mesh):
    whole = P(None, None, "lat", "lon")
    placed = (whole,) + (P(None, "lat", "lon"),) * 8
    body = functools.partial(shards, mesh.shape["lat"], mesh.shape["lon"])
    return jax.shard_map(body, mesh=mesh, in_specs=placed, out_specs=whole, check_vma=False)
```
